32 devices in a mesh: groups: 2 (over y), gx: 16 (over z, x, core).
Axes of the slice: x: 2, y: 2, z: 4, core: 2. Of those that a mesh axis runs over, the one named last changes fastest.
Arguments:
- tokens: bfloat16 [3, 32, 18432], P(None, ('groups', 'gx')), parts along dimension 1, may hold values from -150 to 150
- gain: float32 [18432], replicated, may hold values from 0.5 to 1.5
- w_query: bfloat16 [18432, 12288], P(None, 'gx'), may hold values from -0.046875 to 0.046875
- w_key: bfloat16 [18432, 256], P(None, 'gx'), may hold values from -0.25 to 0.25
- w_value: bfloat16 [18432, 256], P(None, 'gx'), may hold values from -0.046875 to 0.046875
- w_out: bfloat16 [12288, 18432], P(None, 'gx'), may hold values from -0.0546875 to 0.0546875
- cache_keys: bfloat16 [32, 2048, 256], P(('groups', 'gx')), parts along dimension 0, may hold values from -690 to 690
- cache_values: bfloat16 [32, 2048, 256], P(('groups', 'gx')), parts along dimension 0, may hold values from -24 to 24
- lengths: int32 [32], P(('groups', 'gx')), parts along dimension 0, may hold values from 16 to 2048, as said below
- positions: int32 [32], P(('groups', 'gx')), parts along dimension 0, may hold values from 0 to 4095
Outputs:
- layer_out: bfloat16 [3, 32, 18432], P(None, ('groups', 'gx')), parts along dimension 1
The draws below stay inside these ranges and needn't reach their ends.
There are 2 independent parts, one for each index of `groups`. The reference program is written for one: setup_inputs(seed, part) draws one part's arguments, and reference() takes and returns one part's arrays. A program takes and returns all parts, laid end to end along the dimension named above; an argument that names none is the same for every part. Nothing has to cross between parts.
Inputs may be any that keep to these rules, and one draw needn't show every extreme that they name: `lengths`: at least 16 live slots in every row; in every draw some row has all 2048 slots live.
All inputs are finite; a program needn't handle non-finite values.
Results may differ from the reference program's by a relative error of at most 0.0075.
The reference program's roundings to bfloat16 on the way count: a program that leaves them out, or rounds other values in their place, can miss the bound.
Values may be sent and summed in bfloat16 or wider, within the bound.
A program may use at most 192 MiB of HBM per device.

```python
import jax
import jax.numpy as jnp
from jax import lax

D = 18432
HEADS = 48
HD = 256
CACHE = 2048
STEPS = 3
BATCH = 16
QW = 12288


def draw_tokens(key, part):
    key = jax.random.fold_in(key, 11)
    base_key, row_key = jax.random.split(key)
    base = jax.random.truncated_normal(base_key, -5.0, 5.0, (STEPS, BATCH, D), jnp.float32)
    column_scale = 3.0 ** (jnp.arange(D, dtype=jnp.float32) / D)
    row_scale = jnp.exp(jax.random.uniform(row_key, (STEPS, BATCH, 1), jnp.float32, 0.0, 2.3))
    return (base * column_scale * row_scale).astype(jnp.bfloat16)


def draw_cache_keys(key, part):
    key = jax.random.fold_in(key, 12)
    base_key = jax.random.fold_in(key, 0)
    base = 0.5 * jax.random.truncated_normal(base_key, -4.0, 4.0, (BATCH, CACHE, HD), jnp.float32)
    return base.astype(jnp.bfloat16)


def draw_lengths(key, part):
    key = jax.random.fold_in(key, 13)
    value_key, spot_key = jax.random.split(key)
    values = jax.random.randint(value_key, (BATCH,), 16, CACHE + 1, jnp.int32)
    spot = jax.random.randint(spot_key, (), 0, BATCH, jnp.int32)
    index = jnp.arange(BATCH, dtype=jnp.int32)
    values = jnp.where(index == spot, CACHE, values)
    values = jnp.where(index == (spot + 1) % BATCH, 16, values)
    return values.astype(jnp.int32)


def touch_ends(result, stream_key, smallest, high):
    longest = result.shape.index(max(result.shape))
    spots = []
    for shift in (0, 1):
        where = [jax.random.randint(jax.random.fold_in(stream_key, axis), (), 0, length) for axis, length in enumerate(result.shape)]
        where[longest] = (where[longest] + shift) % result.shape[longest]
        spots.append(tuple(where))
    return result.at[spots[0]].set(smallest).at[spots[1]].set(high)


def level_of(key, dims, cuts, low, top_value):
    level = 1.0
    for position, blocks in cuts:
        steps = jax.random.uniform(jax.random.fold_in(jax.random.fold_in(key, 6), position), (blocks,), jnp.float32, low / len(cuts), top_value / len(cuts))
        level = level * jnp.repeat(jnp.exp(steps), dims[position] // blocks).reshape((-1,) + (1,) * (len(dims) - 1 - position))
    return level


def noise(stream_key, shape, deviation, most, shards=(), kind=jnp.bfloat16):
    loudness = level_of(stream_key, shape, shards, -0.22, 0.18) if shards else 1.0
    array = jax.random.normal(stream_key, shape, jnp.float32) * deviation * loudness
    return jnp.minimum(jnp.maximum(array, -most), most).astype(kind)


def setup_inputs(seed: int = 0, part: int = 0) -> dict:
    streams_of = jax.random.split(jax.random.key(seed), 11)
    part_splits = jax.random.split(jax.random.fold_in(streams_of[10], part), 11)
    return {
        "tokens": draw_tokens(jax.random.fold_in(jax.random.fold_in(streams_of[10], part), 71), part),
        "gain": jnp.clip(1.0 + 0.1 * jax.random.normal(streams_of[1], (D,), jnp.float32), 0.5, 1.5),
        "w_query": noise(streams_of[2], (D, QW), D ** -0.5, 0.046875, ((1, 16),)),
        "w_key": noise(streams_of[3], (D, HD), (D // 36) ** -0.5, 0.25, ((1, 16),)),
        "w_value": noise(streams_of[4], (D, HD), D ** -0.5, 0.046875, ((1, 16),)),
        "w_out": noise(streams_of[5], (QW, D), (HEADS * HD) ** -0.5, 0.0546875, ((1, 16),)),
        "cache_keys": draw_cache_keys(jax.random.fold_in(jax.random.fold_in(streams_of[10], part), 71), part),
        "cache_values": noise(part_splits[7], (BATCH, CACHE, HD), 4.0, 24.0, ((0, 16),)),
        "lengths": draw_lengths(jax.random.fold_in(jax.random.fold_in(streams_of[10], part), 71), part),
        "positions": touch_ends(jax.random.randint(part_splits[9], (BATCH,), 0, 4096), jax.random.fold_in(part_splits[9], 1), 0, 4095).astype(jnp.int32),
    }


def rotate(values, where):
    half = values.shape[-1] // 2
    freq = 10000.0 ** (-jnp.arange(half, dtype=jnp.float32) * 2.0 / values.shape[-1])
    angle = where[..., None] * freq
    cosine = jnp.cos(angle)
    sine = jnp.sin(angle)
    first_half = values[..., :half]
    second_half = values[..., half:]
    return jnp.concatenate([first_half * cosine - second_half * sine, second_half * cosine + first_half * sine], axis=-1)

def reference(tokens, gain, w_query, w_key, w_value, w_out, cache_keys, cache_values, lengths, positions):
    scale = 1.0 / HD ** 0.5
    raw_tokens = tokens.astype(jnp.float32)
    row_mean = lax.optimization_barrier(jnp.mean(raw_tokens, axis=-1, keepdims=True))
    row_square = lax.optimization_barrier(jnp.mean(raw_tokens * raw_tokens, axis=-1, keepdims=True))
    row_spread = row_square - row_mean * row_mean
    normed = ((raw_tokens - row_mean) * lax.rsqrt(row_spread + 1e-06) * gain).astype(jnp.bfloat16)
    flat = normed.reshape(STEPS * BATCH, D)
    queries = jnp.dot(flat, w_query, preferred_element_type=jnp.float32).astype(jnp.bfloat16)
    queries = queries.reshape(STEPS, BATCH, HEADS, HD)
    new_keys = jnp.dot(flat, w_key, preferred_element_type=jnp.float32).astype(jnp.bfloat16).reshape(STEPS, BATCH, HD)
    new_values = jnp.dot(flat, w_value, preferred_element_type=jnp.float32).astype(jnp.bfloat16).reshape(STEPS, BATCH, HD)
    step_place = positions[None, :].astype(jnp.float32) + jnp.arange(STEPS, dtype=jnp.float32)[:, None]
    rotated_queries = rotate(queries.astype(jnp.float32), step_place[:, :, None]).astype(jnp.bfloat16)
    rotated_keys = rotate(new_keys.astype(jnp.float32), step_place).astype(jnp.bfloat16)
    causal = jnp.arange(STEPS)[None, :] <= jnp.arange(STEPS)[:, None]

    def one_row(items):
        row_query, row_keys, row_values, stored_keys, stored_values, row_length = items
        query_float = row_query.astype(jnp.float32)
        cache_scores = jnp.einsum('shd,jd->shj', query_float, stored_keys.astype(jnp.float32)) * scale
        live_mask = jnp.arange(CACHE) < row_length
        cache_scores = jnp.where(live_mask[None, None, :], cache_scores, -jnp.inf)
        fresh_scores = jnp.einsum('shd,td->sht', query_float, row_keys.astype(jnp.float32)) * scale
        fresh_scores = jnp.where(causal[:, None, :], fresh_scores, -jnp.inf)
        highest = jnp.maximum(lax.optimization_barrier(jnp.max(cache_scores, axis=-1)), lax.optimization_barrier(jnp.max(fresh_scores, axis=-1)))[..., None]
        cache_exp = jnp.exp(cache_scores - highest)
        fresh_exp = jnp.exp(fresh_scores - highest)
        denominator = lax.optimization_barrier(jnp.sum(cache_exp, axis=-1, keepdims=True)) + lax.optimization_barrier(jnp.sum(fresh_exp, axis=-1, keepdims=True))
        cache_weights = (cache_exp / denominator).astype(jnp.bfloat16)
        fresh_weights = (fresh_exp / denominator).astype(jnp.bfloat16)
        attended = jnp.einsum('shj,jd->shd', cache_weights.astype(jnp.float32), stored_values.astype(jnp.float32))
        attended = attended + jnp.einsum('sht,td->shd', fresh_weights.astype(jnp.float32), row_values.astype(jnp.float32))
        return attended.astype(jnp.bfloat16).reshape(STEPS, HEADS * HD)
    attended = lax.map(one_row, (jnp.transpose(rotated_queries, (1, 0, 2, 3)), jnp.transpose(rotated_keys, (1, 0, 2)), jnp.transpose(new_values, (1, 0, 2)), cache_keys, cache_values, lengths))
    attended = jnp.transpose(attended, (1, 0, 2)).reshape(STEPS * BATCH, HEADS * HD)
    layer_out = jnp.dot(attended, w_out, preferred_element_type=jnp.float32).astype(jnp.bfloat16)
    return layer_out.reshape(STEPS, BATCH, D)
```

```python
import jax
import jax.numpy as jnp
from jax import lax
from jax.sharding import PartitionSpec as P


def rotate(values, where):
    half = values.shape[-1] // 2
    freq = 10000.0 ** (-jnp.arange(half, dtype=jnp.float32) * 2.0 / values.shape[-1])
    angle = where[..., None] * freq
    cosine = jnp.cos(angle)
    sine = jnp.sin(angle)
    first_half = values[..., :half]
    second_half = values[..., half:]
    return jnp.concatenate(
        [first_half * cosine - second_half * sine, second_half * cosine + first_half * sine],
        axis=-1,
    )


def per_device(
    tokens, gain, w_query, w_key, w_value, w_out, cache_keys, cache_values, lengths, positions
):
    step_count, row_count, model_width = tokens.shape
    devices = lax.axis_size("gx")
    query_cols = w_query.shape[1]
    key_cols = w_key.shape[1]
    head_size = cache_keys.shape[2]
    slot_count = cache_keys.shape[1]
    head_count = query_cols * devices // head_size
    scale = 1.0 / head_size**0.5
    row_mean_input = tokens.astype(jnp.float32)
    row_mean = jnp.mean(row_mean_input, axis=-1, keepdims=True)
    row_square = jnp.mean(row_mean_input * row_mean_input, axis=-1, keepdims=True)
    row_spread = row_square - row_mean * row_mean
    normed = ((row_mean_input - row_mean) * lax.rsqrt(row_spread + 1e-06) * gain).astype(
        jnp.bfloat16
    )
    everyone = lax.all_gather(normed, "gx", axis=1, tiled=True)

    def project(weight):
        return jnp.einsum(
            "cbd,de->cbe", everyone, weight, preferred_element_type=jnp.float32
        ).astype(jnp.bfloat16)

    small = jnp.concatenate([project(w_key), project(w_value)], axis=-1)
    query_part = project(w_query)
    together = jnp.concatenate([query_part, small], axis=-1)
    swapped = lax.all_to_all(
        together.reshape(step_count, devices, row_count, -1), "gx", split_axis=1, concat_axis=1
    )
    swapped = jnp.swapaxes(swapped, 1, 2)
    queries = swapped[..., :query_cols].reshape(step_count, row_count, head_count, head_size)
    new_keys = swapped[..., query_cols : query_cols + key_cols].reshape(
        step_count, row_count, head_size
    )
    new_values = swapped[..., query_cols + key_cols :].reshape(step_count, row_count, head_size)
    step_place = (
        positions[None, :].astype(jnp.float32)
        + jnp.arange(step_count).astype(jnp.float32)[:, None]
    )
    rotated_queries = rotate(queries.astype(jnp.float32), step_place[:, :, None]).astype(
        jnp.bfloat16
    )
    rotated_keys = rotate(new_keys.astype(jnp.float32), step_place).astype(jnp.bfloat16)
    live_mask = jnp.arange(slot_count)[None, :] < lengths[:, None]
    cache_scores = (
        jnp.einsum(
            "crhd,rjd->crhj", rotated_queries, cache_keys, preferred_element_type=jnp.float32
        )
        * scale
    )
    cache_scores = jnp.where(live_mask[None, :, None, :], cache_scores, -jnp.inf)
    fresh_scores = (
        jnp.einsum(
            "crhd,trd->crht", rotated_queries, rotated_keys, preferred_element_type=jnp.float32
        )
        * scale
    )
    causal = jnp.arange(step_count)[None, :] <= jnp.arange(step_count)[:, None]
    fresh_scores = jnp.where(causal[:, None, None, :], fresh_scores, -jnp.inf)
    highest = jnp.maximum(jnp.max(cache_scores, axis=-1), jnp.max(fresh_scores, axis=-1))[
        ..., None
    ]
    cache_exp = jnp.exp(cache_scores - highest)
    fresh_exp = jnp.exp(fresh_scores - highest)
    denominator = jnp.sum(cache_exp, axis=-1, keepdims=True) + jnp.sum(
        fresh_exp, axis=-1, keepdims=True
    )
    cache_weights = (cache_exp / denominator).astype(jnp.bfloat16)
    fresh_weights = (fresh_exp / denominator).astype(jnp.bfloat16)
    attended = jnp.einsum(
        "crhj,rjd->crhd", cache_weights, cache_values, preferred_element_type=jnp.float32
    )
    attended = attended + jnp.einsum(
        "crht,trd->crhd", fresh_weights, new_values, preferred_element_type=jnp.float32
    )
    attended = attended.astype(jnp.bfloat16).reshape(
        step_count, row_count, head_count * head_size
    )
    mixed_cols = jnp.einsum(
        "cbq,qd->cbd",
        lax.all_gather(attended, "gx", axis=1, tiled=True),
        w_out,
        preferred_element_type=jnp.float32,
    ).astype(jnp.bfloat16)
    return lax.all_to_all(mixed_cols, "gx", split_axis=1, concat_axis=2, tiled=True)


def solution(mesh):
    in_specs = (
        P(None, ("groups", "gx"), None),
        P(),
        P(None, "gx"),
        P(None, "gx"),
        P(None, "gx"),
        P(None, "gx"),
        P(("groups", "gx"), None, None),
        P(("groups", "gx"), None, None),
        P(("groups", "gx")),
        P(("groups", "gx")),
    )
    out_specs = P(None, ("groups", "gx"), None)
    return jax.shard_map(
        per_device, mesh=mesh, in_specs=in_specs, out_specs=out_specs, check_vma=False
    )
```

```python
import jax
import jax.numpy as jnp
from jax import lax
from jax.experimental import pallas as pl
from jax.experimental.pallas import tpu as pltpu
from jax.sharding import PartitionSpec as P


def rotate(values, where):
    half = values.shape[-1] // 2
    freq = 10000.0 ** (-jnp.arange(half, dtype=jnp.float32) * 2.0 / values.shape[-1])
    angle = where[..., None] * freq
    cosine = jnp.cos(angle)
    sine = jnp.sin(angle)
    first_half = values[..., :half]
    second_half = values[..., half:]
    return jnp.concatenate(
        [first_half * cosine - second_half * sine, second_half * cosine + first_half * sine],
        axis=-1,
    )


def plain_layer(
    tokens, gain, w_query, w_key, w_value, w_out, cache_keys, cache_values, lengths, positions
):
    step_count, row_count, model_width = tokens.shape
    devices = lax.axis_size("gx")
    query_cols = w_query.shape[1]
    key_cols = w_key.shape[1]
    head_size = cache_keys.shape[2]
    slot_count = cache_keys.shape[1]
    head_count = query_cols * devices // head_size
    scale = 1.0 / head_size**0.5
    row_mean_input = tokens.astype(jnp.float32)
    row_mean = jnp.mean(row_mean_input, axis=-1, keepdims=True)
    row_square = jnp.mean(row_mean_input * row_mean_input, axis=-1, keepdims=True)
    row_spread = row_square - row_mean * row_mean
    normed = ((row_mean_input - row_mean) * lax.rsqrt(row_spread + 1e-06) * gain).astype(
        jnp.bfloat16
    )
    everyone = lax.all_gather(normed, "gx", axis=1, tiled=True)

    def project(weight):
        return jnp.einsum(
            "cbd,de->cbe", everyone, weight, preferred_element_type=jnp.float32
        ).astype(jnp.bfloat16)

    small = jnp.concatenate([project(w_key), project(w_value)], axis=-1)
    query_part = project(w_query)
    together = jnp.concatenate([query_part, small], axis=-1)
    swapped = lax.all_to_all(
        together.reshape(step_count, devices, row_count, -1), "gx", split_axis=1, concat_axis=1
    )
    swapped = jnp.swapaxes(swapped, 1, 2)
    queries = swapped[..., :query_cols].reshape(step_count, row_count, head_count, head_size)
    new_keys = swapped[..., query_cols : query_cols + key_cols].reshape(
        step_count, row_count, head_size
    )
    new_values = swapped[..., query_cols + key_cols :].reshape(step_count, row_count, head_size)
    step_place = (
        positions[None, :].astype(jnp.float32)
        + jnp.arange(step_count).astype(jnp.float32)[:, None]
    )
    rotated_queries = rotate(queries.astype(jnp.float32), step_place[:, :, None]).astype(
        jnp.bfloat16
    )
    rotated_keys = rotate(new_keys.astype(jnp.float32), step_place).astype(jnp.bfloat16)
    live_mask = jnp.arange(slot_count)[None, :] < lengths[:, None]
    cache_scores = (
        jnp.einsum(
            "crhd,rjd->crhj", rotated_queries, cache_keys, preferred_element_type=jnp.float32
        )
        * scale
    )
    cache_scores = jnp.where(live_mask[None, :, None, :], cache_scores, -jnp.inf)
    fresh_scores = (
        jnp.einsum(
            "crhd,trd->crht", rotated_queries, rotated_keys, preferred_element_type=jnp.float32
        )
        * scale
    )
    causal = jnp.arange(step_count)[None, :] <= jnp.arange(step_count)[:, None]
    fresh_scores = jnp.where(causal[:, None, None, :], fresh_scores, -jnp.inf)
    highest = jnp.maximum(jnp.max(cache_scores, axis=-1), jnp.max(fresh_scores, axis=-1))[
        ..., None
    ]
    cache_exp = jnp.exp(cache_scores - highest)
    fresh_exp = jnp.exp(fresh_scores - highest)
    denominator = jnp.sum(cache_exp, axis=-1, keepdims=True) + jnp.sum(
        fresh_exp, axis=-1, keepdims=True
    )
    cache_weights = (cache_exp / denominator).astype(jnp.bfloat16)
    fresh_weights = (fresh_exp / denominator).astype(jnp.bfloat16)
    attended = jnp.einsum(
        "crhj,rjd->crhd", cache_weights, cache_values, preferred_element_type=jnp.float32
    )
    attended = attended + jnp.einsum(
        "crht,trd->crhd", fresh_weights, new_values, preferred_element_type=jnp.float32
    )
    attended = attended.astype(jnp.bfloat16).reshape(
        step_count, row_count, head_count * head_size
    )
    mixed_cols = jnp.einsum(
        "cbq,qd->cbd",
        lax.all_gather(attended, "gx", axis=1, tiled=True),
        w_out,
        preferred_element_type=jnp.float32,
    ).astype(jnp.bfloat16)
    return lax.all_to_all(mixed_cols, "gx", split_axis=1, concat_axis=2, tiled=True)


MESH = pl.DeviceIdType.MESH
PEERS = 16
VMEM_BYTES = 64 * 1024 * 1024
PARTS = 3
ACROSS, SIBLING = range(2)


def layer_kernel(
    tokens,
    gain,
    lengths,
    positions,
    wq_hbm,
    wk_hbm,
    wv_hbm,
    wo_hbm,
    keys_hbm,
    values_hbm,
    out,
    wq,
    wkv,
    wo,
    keys,
    values,
    blocks,
    left,
    spread,
    moved,
    acc,
    out_acc,
    rotated,
    sent,
    got,
    sent_out,
    got_out,
    wq_sem,
    wkv_sem,
    wo_sem,
    cache_sem,
    line_sem,
    send_sem,
    recv_sem,
    swap_send,
    swap_recv,
    back_send,
    back_recv,
):
    f32 = jnp.float32
    bf16 = jnp.bfloat16
    steps = 3
    me = lax.axis_index("gx")
    z, x, core = me // 4, (me // 2) % 2, me % 2

    def at(zz, xx, cc):
        return zz * 4 + xx * 2 + cc

    wq_copies = [
        pltpu.make_async_copy(wq_hbm.at[c], wq.at[c], wq_sem.at[c]) for c in range(PARTS)
    ]
    part_len = wkv.shape[2]
    wkv_copies = []
    for c in range(PARTS):
        cols = pl.ds(c * part_len, part_len)
        wkv_copies.append(
            (
                pltpu.make_async_copy(
                    wk_hbm.at[:, cols], wkv.at[c, pl.ds(0, 16), :], wkv_sem.at[c, 0]
                ),
                pltpu.make_async_copy(
                    wv_hbm.at[:, cols], wkv.at[c, pl.ds(16, 16), :], wkv_sem.at[c, 1]
                ),
            )
        )
    wo_copies = [
        pltpu.make_async_copy(wo_hbm.at[:, c], wo.at[c], wo_sem.at[c]) for c in range(PARTS)
    ]
    keys_copy = pltpu.make_async_copy(keys_hbm, keys, cache_sem.at[0])
    values_copy = pltpu.make_async_copy(values_hbm, values, cache_sem.at[1])
    for c in range(PARTS):
        wq_copies[c].start()
        wkv_copies[c][0].start()
        wkv_copies[c][1].start()
    keys_copy.start()
    values_copy.start()
    for c in range(PARTS):
        wo_copies[c].start()

    barrier = pltpu.get_barrier_semaphore()
    for shift in range(1, PEERS):
        pl.semaphore_signal(
            barrier, inc=1, device_id={"gx": (me + shift) % PEERS}, device_id_type=MESH
        )

    width = blocks.shape[3]
    features = PARTS * 16 * width
    raw = tokens[...].astype(f32)
    mean = jnp.sum(raw, axis=1, keepdims=True) * (1.0 / features)
    square = jnp.sum(raw * raw, axis=1, keepdims=True) * (1.0 / features)
    factor = lax.rsqrt(square - mean * mean + 1e-06)
    for c in range(PARTS):
        for u in range(16):
            for group in range(width // 128):
                cols = pl.ds((c * 16 + u) * width + group * 128, 128)
                line = (tokens[:, cols].astype(f32) - mean) * factor * gain[:, cols]
                spread[group, pl.ds(u, steps, 16), :] = line
        for group in range(width // 128):
            blocks[c, me, :, pl.ds(group * 128, 128)] = spread[group, pl.ds(0, 48), :].astype(
                bf16
            )

    pl.semaphore_wait(barrier, PEERS - 1)

    def gather(lanes):
        def copy(c, d, sem, target):
            ref = blocks.at[c, d, :, pl.ds(0, lanes)]
            return pltpu.make_async_remote_copy(
                src_ref=ref,
                dst_ref=ref,
                send_sem=sem,
                recv_sem=recv_sem.at[c, d],
                device_id={"gx": target},
                device_id_type=MESH,
            )

        def up(c, k):
            return copy(c, me, line_sem.at[c, k - 1], at(jnp.minimum(z + k, 3), x, core))

        def down(c, k):
            return copy(c, me, line_sem.at[c, k + 2], at(jnp.maximum(z - k, 0), x, core))

        def across(c, d):
            return copy(c, d, send_sem.at[c, ACROSS, d], at(z, 1 - x, core))

        def sibling(c, d):
            return copy(c, d, send_sem.at[c, SIBLING, d], at(z, x, 1 - core))

        def own(c):
            for k in range(1, 4):
                pl.when(z + k <= 3)(up(c, k).start)
                pl.when(z >= k)(down(c, k).start)
            across(c, me).start()
            sibling(c, me).start()

        def hop(c):
            for k in range(1, 4):
                for near, d in ((z >= k, at(z - k, x, core)), (z + k <= 3, at(z + k, x, core))):

                    @pl.when(near)
                    def _(d=d):
                        sibling(c, d).wait_recv()
                        across(c, d).start()
                        sibling(c, d).start()

        def from_across(c):
            for zz in range(4):
                d = at(zz, 1 - x, core)
                sibling(c, d).wait_recv()
                sibling(c, d).start()

        def from_sibling(c):
            for zz in range(4):
                for xx in range(2):
                    sibling(c, at(zz, xx, 1 - core)).wait_recv()

        def drain(c):
            for k in range(1, 4):
                pl.when(z + k <= 3)(up(c, k).wait_send)
                pl.when(z >= k)(down(c, k).wait_send)
            for zz in range(4):
                mine = at(zz, x, core)
                across(c, mine).wait_send()
                sibling(c, mine).wait_send()
                sibling(c, at(zz, 1 - x, core)).wait_send()

        return own, hop, from_across, from_sibling, drain

    def line_up(c, lanes):
        for t in range(steps):
            for group in range(lanes // 128):
                slot = (t * (lanes // 128) + group) % spread.shape[0]
                cols = pl.ds(group * 128, 128)
                spread[slot] = (
                    blocks[c, :, pl.ds(t * 16, 16), cols].astype(f32).reshape(PEERS * 16, 128)
                )
                for u in range(16):
                    left[pl.ds(t * 16, 16), pl.ds(u * lanes + group * 128, 128)] = spread[
                        slot, pl.ds(u, PEERS, 16), :
                    ].astype(bf16)

    own, hop, from_across, from_sibling, drain = gather(width)
    own(0)
    own(1)
    own(2)
    hop(0)
    hop(1)
    from_across(0)
    hop(2)
    from_across(1)
    tile = 768
    acc_q = jnp.zeros(acc.shape, f32)
    acc_kv = jnp.zeros((48, 32), f32)
    for c in range(PARTS):
        if c == 1:
            from_across(2)
        from_sibling(c)
        line_up(c, width)
        wq_copies[c].wait()
        wkv_copies[c][0].wait()
        wkv_copies[c][1].wait()

        def project(i, carry, c=c):
            acc_q, acc_kv = carry
            span = pl.ds(pl.multiple_of(i * tile, tile), tile)
            part = left[:, span]
            acc_q = acc_q + jnp.dot(part, wq[c, span, :], preferred_element_type=f32)
            acc_kv = acc_kv + lax.dot_general(
                part, wkv[c, :, span], (((1,), (1,)), ((), ())), preferred_element_type=f32
            )
            return acc_q, acc_kv

        acc_q, acc_kv = lax.fori_loop(0, part_len // tile, project, (acc_q, acc_kv))
    for c in range(PARTS):
        drain(c)

    acc[...] = acc_q
    place_row = lax.broadcasted_iota(jnp.int32, (32, 256), 0)
    place_col = lax.broadcasted_iota(jnp.int32, (32, 256), 1)
    small = acc_kv.astype(bf16)
    place_k = (place_col == me * 16 + place_row) & (place_row < 16)
    place_v = (place_col == me * 16 + place_row - 16) & (place_row >= 16)
    full_k = jnp.dot(
        small, place_k.astype(f32).astype(bf16), preferred_element_type=f32
    )
    full_v = jnp.dot(
        small, place_v.astype(f32).astype(bf16), preferred_element_type=f32
    )
    for half in range(2):
        base = half * 256
        for t in range(steps):
            rows = slice(t * 16, t * 16 + 16)
            for h in range(3):
                moved[pl.ds(base + t * 3 + h, 16, 16), :] = acc[
                    rows, pl.ds(h * 256 + half * 128, 128)
                ]
            cols = slice(half * 128, half * 128 + 128)
            moved[pl.ds(base + 9 + t, 16, 16), :] = full_k[rows, cols]
            moved[pl.ds(base + 12 + t, 16, 16), :] = full_v[rows, cols]
        moved[pl.ds(base + 15, 16, 16), :] = jnp.zeros((16, 128), f32)
    for half in range(2):
        sent[:, :, pl.ds(half * 128, 128)] = (
            moved[pl.ds(half * 256, 256), :].reshape(PEERS, 16, 128).astype(bf16)
        )

    def swap(source, target, send_sems, recv_sems, shift):
        to = (me + shift) % PEERS
        origin = (me + PEERS - shift) % PEERS
        out_copy = pltpu.make_async_remote_copy(
            src_ref=source.at[to],
            dst_ref=target.at[me],
            send_sem=send_sems.at[shift],
            recv_sem=recv_sems.at[shift],
            device_id={"gx": to},
            device_id_type=MESH,
        )
        in_copy = pltpu.make_async_remote_copy(
            src_ref=source.at[to],
            dst_ref=target.at[origin],
            send_sem=send_sems.at[shift],
            recv_sem=recv_sems.at[shift],
            device_id={"gx": to},
            device_id_type=MESH,
        )
        return out_copy, in_copy

    swaps = [swap(sent, got, swap_send, swap_recv, shift) for shift in range(1, PEERS)]
    for out_copy, _ in swaps:
        out_copy.start()
    got[me] = sent[me]

    lane = lax.broadcasted_iota(jnp.int32, (8, 128), 1).astype(f32)
    step = lax.broadcasted_iota(jnp.int32, (8, 128), 0).astype(f32)
    freq = jnp.exp(lane * (-2.0 / 256.0) * 9.210340371976184)
    angle = (positions[0].astype(f32) + step) * freq
    cosine = jnp.cos(angle)
    sine = jnp.sin(angle)
    keys_copy.wait()
    values_copy.wait()
    for out_copy, in_copy in swaps:
        in_copy.wait_recv()

    for half in range(2):
        moved[pl.ds(half * 256, 256), :] = (
            got[:, :, pl.ds(half * 128, 128)].astype(f32).reshape(256, 128)
        )
    key_rows = []
    value_rows = []
    for t in range(steps):
        cos_t = cosine[t : t + 1]
        sin_t = sine[t : t + 1]
        for h in range(3):
            first = moved[pl.ds(t * 3 + h, 16, 16), :]
            second = moved[pl.ds(256 + t * 3 + h, 16, 16), :]
            rows = pl.ds(t * 16, 16)
            rotated[h, rows, pl.ds(0, 128)] = (first * cos_t - second * sin_t).astype(bf16)
            rotated[h, rows, pl.ds(128, 128)] = (second * cos_t + first * sin_t).astype(bf16)
        first = jnp.sum(moved[pl.ds(9 + t, 16, 16), :], axis=0, keepdims=True)
        second = jnp.sum(moved[pl.ds(256 + 9 + t, 16, 16), :], axis=0, keepdims=True)
        key_rows.append((first * cos_t - second * sin_t, second * cos_t + first * sin_t))
        value_rows.append(
            tuple(
                jnp.sum(moved[pl.ds(base + 12 + t, 16, 16), :], axis=0, keepdims=True)
                for base in (0, 256)
            )
        )
    place = lax.broadcasted_iota(jnp.int32, (16, 128), 0)

    def stack(rows):
        halves = []
        for half in range(2):
            stacked = jnp.zeros((16, 128), f32)
            for t in range(steps):
                stacked = jnp.where(place == t, rows[t][half], stacked)
            halves.append(stacked)
        return jnp.concatenate(halves, axis=1).astype(bf16)

    fresh_keys = stack(key_rows)
    fresh_values = stack(value_rows)

    slots = keys.shape[0]
    live = lax.broadcasted_iota(jnp.int32, (48, slots), 1) < lengths[0]
    row_step = lax.broadcasted_iota(jnp.int32, (48, 16), 0) // 16
    causal = lax.broadcasted_iota(jnp.int32, (48, 16), 1) <= row_step
    over = (((1,), (1,)), ((), ()))

    def attend(h):
        query = rotated[h]
        score = lax.dot_general(query, keys[...], over, preferred_element_type=f32) * 0.0625
        score = jnp.where(live, score, -jnp.inf)
        fresh = lax.dot_general(query, fresh_keys, over, preferred_element_type=f32) * 0.0625
        fresh = jnp.where(causal, fresh, -jnp.inf)
        highest = jnp.maximum(
            jnp.max(score, axis=1, keepdims=True), jnp.max(fresh, axis=1, keepdims=True)
        )
        score = jnp.exp(score - highest)
        fresh = jnp.exp(fresh - highest)
        whole = jnp.sum(score, axis=1, keepdims=True) + jnp.sum(fresh, axis=1, keepdims=True)
        share = 1.0 / whole
        result = jnp.dot(
            (score * share).astype(bf16), values[...], preferred_element_type=f32
        ) + jnp.dot((fresh * share).astype(bf16), fresh_values, preferred_element_type=f32)
        blocks[h, me, :, pl.ds(0, 256)] = result.astype(bf16)

    own, hop, from_across, from_sibling, drain = gather(256)
    attend(0)
    own(0)
    attend(1)
    own(1)
    attend(2)
    own(2)
    hop(0)
    hop(1)
    from_across(0)
    hop(2)
    from_across(1)
    depth = 4
    for c in range(PARTS):
        if c == 1:
            from_across(2)
        from_sibling(c)
        line_up(c, 256)
        wo_copies[c].wait()

        def mix(i, carry, c=c):
            part = left[:, pl.ds(pl.multiple_of(i * depth * 256, 1024), depth * 256)]
            weight = wo[c, pl.ds(i * depth, depth)].reshape(depth * 256, out_acc.shape[1])
            out_acc[...] += jnp.dot(part, weight, preferred_element_type=f32)
            return carry

        if c == 0:
            out_acc[...] = jnp.zeros(out_acc.shape, f32)
        lax.fori_loop(0, 16 // depth, mix, 0)
    for c in range(PARTS):
        drain(c)
    for out_copy, _ in swaps:
        out_copy.wait_send()

    groups = out_acc.shape[1] // 128
    for t in range(steps):
        for group in range(groups):
            moved[pl.ds(t * groups + group, 16, 32), :] = out_acc[
                pl.ds(t * 16, 16), pl.ds(group * 128, 128)
            ]
    for spare in range(steps * groups, 32):
        moved[pl.ds(spare, 16, 32), :] = jnp.zeros((16, 128), f32)
    sent_out[...] = moved[...].reshape(PEERS, 32, 128).astype(bf16)
    backs = [swap(sent_out, got_out, back_send, back_recv, shift) for shift in range(1, PEERS)]
    for out_copy, _ in backs:
        out_copy.start()
    got_out[me] = sent_out[me]
    for _, in_copy in backs:
        in_copy.wait_recv()
    moved[...] = got_out[...].astype(f32).reshape(PEERS * 32, 128)
    for source in range(PEERS):
        for group in range(groups):
            out[:, pl.ds((source * groups + group) * 128, 128)] = moved[
                pl.ds(source * 32 + group, steps, groups), :
            ].astype(bf16)
    for out_copy, _ in backs:
        out_copy.wait_send()


def layer(
    tokens, gain, w_query, w_key, w_value, w_out, cache_keys, cache_values, lengths, positions
):
    step_count, row_count, model_width = tokens.shape
    devices = lax.axis_size("gx")
    query_cols = w_query.shape[1]
    key_cols = w_key.shape[1]
    out_cols = w_out.shape[1]
    head_size = cache_keys.shape[2]
    slot_count = cache_keys.shape[1]
    fits = (
        devices == PEERS
        and (step_count, row_count, head_size) == (3, 1, 256)
        and (query_cols, key_cols) == (3 * head_size, 16)
        and out_cols % 128 == 0
        and step_count * out_cols <= 32 * 128
        and model_width == devices * out_cols
        and model_width % (PARTS * 16 * 384) == 0
        and w_out.shape[0] == devices * query_cols
    )
    if not fits:
        return plain_layer(
            tokens,
            gain,
            w_query,
            w_key,
            w_value,
            w_out,
            cache_keys,
            cache_values,
            lengths,
            positions,
        )
    part_len = model_width // PARTS
    width = part_len // 16
    bf16 = jnp.bfloat16
    f32 = jnp.float32
    vmem = pl.BlockSpec(memory_space=pltpu.VMEM)
    smem = pl.BlockSpec(memory_space=pltpu.SMEM)
    hbm = pl.BlockSpec(memory_space=pl.ANY)
    dma = pltpu.SemaphoreType.DMA
    result = pl.pallas_call(
        layer_kernel,
        out_shape=jax.ShapeDtypeStruct((step_count, model_width), bf16),
        in_specs=[vmem, vmem, smem, smem] + [hbm] * 6,
        out_specs=vmem,
        scratch_shapes=[
            pltpu.VMEM((PARTS, part_len, query_cols), bf16),
            pltpu.VMEM((PARTS, 2 * key_cols, part_len), bf16),
            pltpu.VMEM((PARTS, 16, head_size, out_cols), bf16),
            pltpu.VMEM((slot_count, head_size), bf16),
            pltpu.VMEM((slot_count, head_size), bf16),
            pltpu.VMEM((PARTS, PEERS, 48, width), bf16),
            pltpu.VMEM((48, part_len), bf16),
            pltpu.VMEM((3, PEERS * 16, 128), f32),
            pltpu.VMEM((PEERS * 32, 128), f32),
            pltpu.VMEM((48, query_cols), f32),
            pltpu.VMEM((48, out_cols), f32),
            pltpu.VMEM((3, 48, head_size), bf16),
            pltpu.VMEM((PEERS, 16, head_size), bf16),
            pltpu.VMEM((PEERS, 16, head_size), bf16),
            pltpu.VMEM((PEERS, 32, 128), bf16),
            pltpu.VMEM((PEERS, 32, 128), bf16),
            dma((PARTS,)),
            dma((PARTS, 2)),
            dma((PARTS,)),
            dma((2,)),
            dma((PARTS, 6)),
            dma((PARTS, 2, PEERS)),
            dma((PARTS, PEERS)),
            dma((PEERS,)),
            dma((PEERS,)),
            dma((PEERS,)),
            dma((PEERS,)),
        ],
        compiler_params=pltpu.CompilerParams(
            collective_id=0, has_side_effects=True, vmem_limit_bytes=VMEM_BYTES
        ),
    )(
        tokens.reshape(step_count, model_width),
        gain.reshape(1, model_width),
        lengths,
        positions,
        w_query.reshape(PARTS, part_len, query_cols),
        w_key.T,
        w_value.T,
        w_out.reshape(16, PARTS, head_size, out_cols),
        cache_keys.reshape(slot_count, head_size),
        cache_values.reshape(slot_count, head_size),
    )
    return result.reshape(step_count, 1, model_width)


def solution(mesh):
    in_specs = (
        P(None, ("groups", "gx"), None),
        P(),
        P(None, "gx"),
        P(None, "gx"),
        P(None, "gx"),
        P(None, "gx"),
        P(("groups", "gx"), None, None),
        P(("groups", "gx"), None, None),
        P(("groups", "gx")),
        P(("groups", "gx")),
    )
    out_specs = P(None, ("groups", "gx"), None)
    return jax.shard_map(
        layer, mesh=mesh, in_specs=in_specs, out_specs=out_specs, check_vma=False
    )
```
